32 devices in a mesh: node: 8 (over z, x), local: 4 (over y, core).
Axes of the slice: x: 2, y: 2, z: 4, core: 2. Of those that a mesh axis runs over, the one named last changes fastest.
Arguments:
- tokens: bfloat16 [512, 7168], P(('node', 'local')), may hold values from -6 to 6
- expert_ids: int32 [512, 2], P(('node', 'local')), may hold values from 0 to 7, all different within a row; in each aligned block of 16 rows (0 to 15, 16 to 31, ...) at most 4 rows name the same one
- combine_weights: float32 [512, 2], P(('node', 'local')), may hold values from 0.25 to 1
- w_gate: bfloat16 [8, 7168, 1024], P('node', None, 'local'), may hold values from -0.0625 to 0.0625
- w_up: bfloat16 [8, 7168, 1024], P('node', None, 'local'), may hold values from -0.0625 to 0.0625
- w_down: bfloat16 [8, 1024, 7168], P('node', 'local'), may hold values from -0.1875 to 0.1875
Outputs:
- moe_out: bfloat16 [512, 7168], P(('node', 'local'))
The draws below stay inside these ranges and needn't reach their ends.
Inputs may be any that keep to these rules, and one draw needn't show every extreme that they name: `expert_ids`: each row names 2 different experts. Among the 16 rows of one device no expert is named more than 4 times, and in every draw some expert is named exactly 4 times by the rows of some device.
All inputs are finite; a program needn't handle non-finite values.
Results may differ from the reference program's by a relative error of at most 0.0095.
Values may be sent and summed in bfloat16 or wider, within the bound.
A program may use at most 64 MiB of HBM per device.

```python
import math
import jax
import jax.numpy as jnp
import numpy as np
from jax import lax

D = 7168
H_DEV = 256
TOK_DEV = 16
TOP = 2
FF = 1024
EXPERTS = 8
CAP = 4
TOKENS = 512
N_LOCAL = 4


def shard_levels(own_key, shape, pieces, least, top_value):
    gain = 1.0
    for dim, parts in pieces:
        heights = jax.random.uniform(jax.random.fold_in(jax.random.fold_in(own_key, 6), dim), (parts,), jnp.float32, least / len(pieces), top_value / len(pieces))
        gain = gain * jnp.repeat(jnp.exp(heights), shape[dim] // parts).reshape((-1,) + (1,) * (len(shape) - 1 - dim))
    return gain


def deal_out(key, own, number, rows, count, top, bound, slope):
    sequence = jax.random.permutation(key, count)
    packed, usual = load_shares(count, rows * top, bound, slope, True), load_shares(count, rows * top, bound, slope, False)
    places = jnp.arange(count)

    def named(sizes, turn):
        used = int((sizes > 0).sum())
        fixed = max(1, used // 4)
        shifted = fixed + (places - fixed + turn * (used - fixed)) % max(1, count - fixed)
        return jnp.zeros((count,), jnp.int32).at[sequence[jnp.where(places < fixed, places, shifted)]].set(jnp.asarray(sizes, jnp.int32))

    sizes = jnp.where(number % 4 == 0, named(packed, number // 4), named(usual, number - number // 4 - 1))
    mixed = jax.random.permutation(jax.random.fold_in(own, 3), count)
    giver, receiver = mixed[0:count // 2 * 2:2], mixed[1:count // 2 * 2:2]
    margin = jnp.minimum(sizes[giver] - 1, bound - sizes[receiver]) // 2
    margin = jnp.where((giver == sequence[0]) | (receiver == sequence[0]) | (sizes[receiver] == 0), 0, jnp.maximum(margin, 0))
    shifted = jax.random.randint(jax.random.fold_in(own, 4), (count // 2,), 0, 1 << 20) % (margin + 1)
    sizes = sizes.at[giver].add(-shifted).at[receiver].add(shifted)
    labels = jnp.searchsorted(jnp.cumsum(sizes), jnp.arange(rows * top), side="right").astype(jnp.int32)
    table = labels.reshape(top, rows).T
    table = table[jax.random.permutation(jax.random.fold_in(own, 1), rows)]
    turn = jax.random.randint(jax.random.fold_in(own, 2), (rows, 1), 0, top)
    return jnp.take_along_axis(table, (jnp.arange(top)[None, :] + turn) % top, axis=1)


def load_shares(amount, total, limit, slope, full):
    weights = [(1 << 20) // math.isqrt(standing ** slope) + 1 for standing in range(1, amount + 1)]
    largest = limit if full else min(limit, max(-(-total // amount), total * weights[0] // sum(weights)))
    least = 1 if total - largest >= amount - 1 else 0
    given, rest = [largest] + [least] * (amount - 1), total - largest - least * (amount - 1)
    while rest > 0:
        movable = [i for i in range(1, amount) if given[i] < largest] or [i for i in range(1, amount) if given[i] < limit]
        mass, remaining = sum([weights[i] for i in movable]), rest
        for i in movable:
            addition = min(limit - given[i], max(1, remaining * weights[i] // mass), rest)
            given[i] = given[i] + addition
            rest = rest - addition
    return np.array(given)


def centred(stream_key, extent, width, bound, pieces=(), kind=jnp.bfloat16):
    gain = shard_levels(stream_key, extent, pieces, -0.22, 0.18) if pieces else 1.0
    values = jax.random.normal(stream_key, extent, jnp.float32) * width * gain
    return jnp.minimum(jnp.maximum(values, -bound), bound).astype(kind)


def setup_inputs(seed: int = 0) -> dict:
    key_list = jax.random.split(jax.random.key(seed), 7)
    tokens = centred(key_list[0], (TOKENS, D), 1.0, 6.0, ((0, 32),))
    expert_ids_keys = jax.random.split(jax.random.fold_in(key_list[1], 1), TOKENS // TOK_DEV)
    expert_ids_turns = jax.random.permutation(jax.random.fold_in(key_list[1], 3), TOKENS // TOK_DEV)
    expert_ids = jax.vmap(lambda own, number: deal_out(jax.random.fold_in(key_list[1], 2), own, number, TOK_DEV, EXPERTS, TOP, CAP, 2))(expert_ids_keys, expert_ids_turns).reshape((TOKENS, TOP))
    combine_weights = jnp.clip(0.25 + 0.75 * jax.random.uniform(key_list[2], (TOKENS, TOP), jnp.float32) ** shard_levels(key_list[2], (TOKENS, TOP), ((0, 32),), -0.2, 0.2), 0.25, 1.0)
    w_gate = centred(key_list[3], (EXPERTS, D, FF), D ** -0.5, 0.0625, ((0, 8), (2, 4)))
    w_up = centred(key_list[4], (EXPERTS, D, FF), D ** -0.5, 0.0625, ((0, 8), (2, 4)))
    w_down = centred(key_list[5], (EXPERTS, FF, D), FF ** -0.5, 0.1875, ((0, 8), (1, 4)))
    return dict(tokens=tokens, expert_ids=expert_ids, combine_weights=combine_weights, w_gate=w_gate, w_up=w_up, w_down=w_down)


def reference(tokens, expert_ids, combine_weights, w_gate, w_up, w_down):
    pairs = TOKENS * TOP
    flat_ids = expert_ids.reshape(-1).astype(jnp.int32)
    token_of = (jnp.arange(pairs, dtype=jnp.int32) // TOP).astype(jnp.int32)
    onehot = (flat_ids[:, None] == jnp.arange(EXPERTS, dtype=jnp.int32)[None, :]).astype(jnp.int32)
    before = jnp.cumsum(onehot, axis=0) - onehot
    slot_of = jnp.sum(before * onehot, axis=1).astype(jnp.int32)
    counts = jnp.sum(onehot, axis=0).astype(jnp.int32)
    padded = ((counts + 127) // 128 * 128).astype(jnp.int32)
    offsets = (jnp.cumsum(padded) - padded).astype(jnp.int32)
    target = (offsets[flat_ids] + slot_of).astype(jnp.int32)
    blocks = pairs // 128 + EXPERTS
    gathered = jnp.zeros((blocks * 128, D), jnp.bfloat16).at[target].set(tokens[token_of])
    block_start = jnp.arange(blocks, dtype=jnp.int32) * 128
    block_expert = jnp.sum((offsets[None, :] <= block_start[:, None]).astype(jnp.int32), axis=1) - 1
    block_expert = jnp.clip(block_expert, 0, EXPERTS - 1).astype(jnp.int32)

    def per_block(operands):
        rows, expert = operands
        gated = jnp.dot(rows, w_gate[expert], preferred_element_type=jnp.float32)
        upward = jnp.dot(rows, w_up[expert], preferred_element_type=jnp.float32)
        hidden = (jax.nn.silu(gated) * upward).astype(jnp.bfloat16)
        split_hidden = hidden.reshape(128, N_LOCAL, H_DEV).astype(jnp.float32)
        split_down = w_down[expert].reshape(N_LOCAL, H_DEV, D).astype(jnp.float32)
        partial_value = jnp.einsum("rlh,lhd->lrd", split_hidden, split_down).astype(jnp.bfloat16)
        return jnp.sum(partial_value.astype(jnp.float32), axis=0).astype(jnp.bfloat16)

    outputs = lax.map(per_block, (gathered.reshape(blocks, 128, D), block_expert))
    outputs = outputs.reshape(blocks * 128, D)
    picked = outputs[target].astype(jnp.float32).reshape(TOKENS, TOP, D)
    mixed = jnp.sum(picked * combine_weights[:, :, None], axis=1)
    return mixed.astype(jnp.bfloat16)
```

```python
import functools
import jax
import jax.numpy as jnp
from jax import lax
from jax.experimental import pallas as pl
from jax.experimental.pallas import tpu as pltpu
from jax.sharding import PartitionSpec as P

CAP = 4
MESH = pl.DeviceIdType.MESH


def flip(index, mask):
    bit = 1
    total = index
    while bit <= mask:
        if mask & bit:
            total = total + bit * (1 - 2 * lax.rem(index // bit, 2))
        bit *= 2
    return total


def kernel(
    nodes, chips, order, groups,
    tok_ref, ids_ref, wts_ref, gate_hbm, up_hbm, down_hbm, out_ref,
    gate, up, down, outgoing, arrived, hidden, partial, from_core, chip_sum, from_chip, expert_out, back,
    w_sem, s_node, r_node, s_core, r_core, s_chip, r_chip, s_fwd, r_fwd,
    s_core2, r_core2, s_chip2, r_chip2, s_node2, r_node2,
):
    width = tok_ref.shape[1]
    rows = tok_ref.shape[0]
    units = gate.shape[1]
    slots = CAP
    pieces = 4
    step = width // pieces
    columns = [slice(q * step, (q + 1) * step) for q in range(pieces)]
    n = lax.axis_index("node")
    l = lax.axis_index("local")
    y = l // 2
    c = lax.rem(l, 2)
    oc = 1 - c

    loads = [
        pltpu.make_async_copy(src.at[0], dst, w_sem.at[i])
        for i, (src, dst) in enumerate(((gate_hbm, gate), (up_hbm, up), (down_hbm, down)))
    ]
    for load in loads:
        load.start()

    def chip_at(step_y):
        return lax.rem(y + step_y, chips)

    def dev(node, chip, core):
        return (node, chip * 2 + core)

    barrier = pltpu.get_barrier_semaphore()
    peers = [dev(flip(n, k), y, c) for k in order if k]
    peers += [dev(n, y, oc)] + [dev(n, chip_at(d), c) for d in range(1, chips)]
    for peer in peers:
        pl.semaphore_signal(barrier, inc=1, device_id=peer, device_id_type=MESH)

    ids = ids_ref[...]
    wts = wts_ref[...]
    places = nodes * slots
    place = lax.broadcasted_iota(jnp.int32, (rows, places), 1)
    first = ids[:, 0:1] == place // slots
    second = ids[:, 1:2] == place // slots
    named = jnp.where(first | second, 1.0, 0.0)
    lower = jnp.where(
        lax.broadcasted_iota(jnp.int32, (rows, rows), 1)
        < lax.broadcasted_iota(jnp.int32, (rows, rows), 0), 1.0, 0.0,
    )
    rank = jnp.dot(lower, named, preferred_element_type=jnp.float32)
    chosen = jnp.where(rank == lax.rem(place, slots).astype(jnp.float32), named, 0.0)
    weight = chosen * jnp.where(first, wts[:, 0:1], wts[:, 1:2])
    weight_hi = weight.astype(jnp.bfloat16)
    weight_lo = (weight - weight_hi.astype(jnp.float32)).astype(jnp.bfloat16)
    chosen = chosen.astype(jnp.bfloat16)
    for cols in columns:
        sent = lax.dot_general(
            chosen, tok_ref[:, cols], (((0,), (0,)), ((), ())),
            preferred_element_type=jnp.float32,
        )
        outgoing[:, :, cols] = sent.astype(jnp.bfloat16).reshape(nodes, slots, step)
    mine = c * chips + y
    p_own = order.index(0)
    arrived[p_own, c, y] = outgoing[n]

    pl.semaphore_wait(barrier, len(peers))

    def remote(src, dst, s_sem, r_sem, to):
        return pltpu.make_async_remote_copy(
            src_ref=src, dst_ref=dst, send_sem=s_sem, recv_sem=r_sem,
            device_id=to, device_id_type=MESH,
        )

    started = []

    def go(copy):
        copy.start()
        started.append(copy)

    def node_copy(p):
        to = flip(n, order[p])
        return remote(outgoing.at[to], arrived.at[p, c, y], s_node.at[p], r_node.at[p], dev(to, y, c))

    for p in reversed(range(nodes)):
        if p != p_own:
            go(node_copy(p))

    def core_copy(p):
        slab = arrived.at[p, c, y]
        return remote(slab, slab, s_core.at[p], r_core.at[p], dev(n, y, oc))

    def chip_copy(p, d):
        slab = arrived.at[p, c, y]
        return remote(slab, slab, s_chip.at[d - 1, p], r_chip.at[d - 1, p], dev(n, chip_at(d), c))

    def chip_arrival(p, d):
        slab = arrived.at[p, c, chip_at(chips - d)]
        return remote(slab, slab, s_chip.at[d - 1, p], r_chip.at[d - 1, p], dev(n, chip_at(d), c))

    def fwd_copy(p, d):
        slab = arrived.at[p, c, chip_at(chips - d)]
        return remote(slab, slab, s_fwd.at[d - 1, p], r_fwd.at[d - 1, p], dev(n, y, oc))

    def fwd_arrival(p, d):
        slab = arrived.at[p, oc, chip_at(chips - d)]
        return remote(slab, slab, s_fwd.at[d - 1, p], r_fwd.at[d - 1, p], dev(n, y, oc))

    def spread(p):
        if p != p_own:
            node_copy(p).wait_recv()
        for d in range(1, chips):
            go(chip_copy(p, d))
        go(core_copy(p))

    def forward(p):
        for d in range(1, chips):
            chip_arrival(p, d).wait_recv()
            go(fwd_copy(p, d))

    def core_copy2(p):
        return remote(partial.at[p, oc], from_core.at[p], s_core2.at[p], r_core2.at[p], dev(n, y, oc))

    def compute(lo, hi):
        for p in range(lo, hi):
            slab = arrived.at[p, oc, y]
            remote(slab, slab, s_core.at[p], r_core.at[p], dev(n, y, oc)).wait_recv()
            for d in range(1, chips):
                fwd_arrival(p, d).wait_recv()
        count = (hi - lo) * 2 * chips * slots
        gated = jnp.zeros((count, units), jnp.float32)
        upward = jnp.zeros((count, units), jnp.float32)
        if lo == 0:
            loads[0].wait()
            loads[1].wait()
        for cols in columns:
            x = arrived[lo:hi, :, :, :, cols].reshape(count, step)
            gated += jnp.dot(x, gate[cols, :], preferred_element_type=jnp.float32)
            upward += jnp.dot(x, up[cols, :], preferred_element_type=jnp.float32)
        hidden[0:count] = (gated / (1.0 + jnp.exp(-gated)) * upward).astype(jnp.bfloat16)
        if lo == 0:
            loads[2].wait()
        for cols in columns:
            value = jnp.dot(hidden[0:count], down[:, cols], preferred_element_type=jnp.float32)
            partial[lo:hi, :, :, :, cols] = value.astype(jnp.bfloat16).reshape(
                hi - lo, 2, chips, slots, step
            )
        for p in range(lo, hi):
            go(core_copy2(p))

    def chip_copy2(p, d):
        return remote(
            chip_sum.at[p, d - 1], from_chip.at[p, d - 1], s_chip2.at[d - 1, p], r_chip2.at[d - 1, p],
            dev(n, chip_at(d), c),
        )

    def to_chips(p):
        core_copy2(p).wait_recv()
        for d in range(1, chips):
            other = chip_at(d)
            both = partial[p, c, other].astype(jnp.float32) + from_core[p, other].astype(jnp.float32)
            chip_sum[p, d - 1] = both.astype(jnp.bfloat16)
            go(chip_copy2(p, d))

    def node_copy2(p):
        return remote(
            expert_out.at[p], back.at[n], s_node2.at[p], r_node2.at[p], dev(flip(n, order[p]), y, c)
        )

    def to_nodes(p):
        total = partial[p, c, y].astype(jnp.float32) + from_core[p, y].astype(jnp.float32)
        for d in range(1, chips):
            chip_copy2(p, d).wait_recv()
            total += from_chip[p, d - 1].astype(jnp.float32)
        if p == p_own:
            back[n] = total.astype(jnp.bfloat16)
        else:
            expert_out[p] = total.astype(jnp.bfloat16)
            go(node_copy2(p))

    lag = 2
    for p in range(nodes + lag):
        if p < nodes:
            spread(p)
        if p >= lag:
            forward(p - lag)
    bounds = [(i * nodes // groups, (i + 1) * nodes // groups) for i in range(groups)]
    for lo, hi in bounds:
        compute(lo, hi)
        for p in range(lo, hi):
            to_chips(p)
    for p in range(nodes):
        to_nodes(p)
    for p in range(nodes):
        if p != p_own:
            src = flip(n, order[p])
            remote(
                expert_out.at[p], back.at[src], s_node2.at[p], r_node2.at[p], dev(src, y, c)
            ).wait_recv()
    for cols in columns:
        rows_back = back[:, :, cols].reshape(places, step)
        mixed = jnp.dot(weight_hi, rows_back, preferred_element_type=jnp.float32)
        mixed += jnp.dot(weight_lo, rows_back, preferred_element_type=jnp.float32)
        out_ref[:, cols] = mixed.astype(jnp.bfloat16)
    for copy in started:
        copy.wait_send()


def body(nodes, chips, tokens, expert_ids, combine_weights, w_gate, w_up, w_down):
    rows, width = tokens.shape
    units = w_gate.shape[2]
    order = sorted(range(nodes), key=lambda k: (k.bit_count(), k))
    groups = 2
    slab = (CAP, width)
    bf = jnp.bfloat16
    sems = pltpu.SemaphoreType.DMA
    vmem = pl.BlockSpec(memory_space=pltpu.VMEM)
    hbm = pl.BlockSpec(memory_space=pl.ANY)
    return pl.pallas_call(
        functools.partial(kernel, nodes, chips, order, groups),
        out_shape=jax.ShapeDtypeStruct((rows, width), bf),
        in_specs=[vmem, vmem, vmem, hbm, hbm, hbm],
        out_specs=vmem,
        scratch_shapes=[
            pltpu.VMEM((width, units), bf),
            pltpu.VMEM((width, units), bf),
            pltpu.VMEM((units, width), bf),
            pltpu.VMEM((nodes,) + slab, bf),
            pltpu.VMEM((nodes, 2, chips) + slab, bf),
            pltpu.VMEM((nodes * 2 * chips * CAP, units), bf),
            pltpu.VMEM((nodes, 2, chips) + slab, bf),
            pltpu.VMEM((nodes, chips) + slab, bf),
            pltpu.VMEM((nodes, chips - 1) + slab, bf),
            pltpu.VMEM((nodes, chips - 1) + slab, bf),
            pltpu.VMEM((nodes,) + slab, bf),
            pltpu.VMEM((nodes,) + slab, bf),
            sems((3,)),
            sems((nodes,)), sems((nodes,)),
            sems((nodes,)), sems((nodes,)),
            sems((chips - 1, nodes)), sems((chips - 1, nodes)),
            sems((chips - 1, nodes)), sems((chips - 1, nodes)),
            sems((nodes,)), sems((nodes,)),
            sems((chips - 1, nodes)), sems((chips - 1, nodes)),
            sems((nodes,)), sems((nodes,)),
        ],
        compiler_params=pltpu.CompilerParams(
            collective_id=0, has_side_effects=True, vmem_limit_bytes=56 * 1024 * 1024
        ),
        name="routed_experts",
    )(tokens, expert_ids, combine_weights, w_gate, w_up, w_down)


def solution(mesh):
    nodes = mesh.shape["node"]
    chips = mesh.shape["local"] // 2
    return jax.shard_map(
        functools.partial(body, nodes, chips),
        mesh=mesh,
        in_specs=(
            P(("node", "local"), None),
            P(("node", "local"), None),
            P(("node", "local"), None),
            P("node", None, "local"),
            P("node", None, "local"),
            P("node", "local", None),
        ),
        out_specs=P(("node", "local"), None),
        check_vma=False,
    )
```

```python
import functools
import jax
import jax.numpy as jnp
from jax import lax
from jax.experimental import pallas as pl
from jax.experimental.pallas import tpu as pltpu
from jax.sharding import PartitionSpec as P

CAP = 4
MESH = pl.DeviceIdType.MESH


def flip(index, mask):
    bit = 1
    total = index
    while bit <= mask:
        if mask & bit:
            total = total + bit * (1 - 2 * lax.rem(index // bit, 2))
        bit *= 2
    return total


def kernel(
    nodes, chips, order, early, way_back, groups, windows,
    tok_ref, ids_ref, wts_ref, gate_hbm, up_hbm, down_hbm, out_ref,
    gate, up, down, outgoing, arrived, hidden, partial, from_core, chip_sum, from_chip, expert_out, back,
    w_sem, s_node, r_node, s_core, r_core, s_chip, r_chip, s_fwd, r_fwd,
    s_core2, r_core2, s_chip2, r_chip2, s_node2, r_node2,
):
    width = tok_ref.shape[1]
    rows = tok_ref.shape[0]
    units = gate.shape[1]
    slots = CAP
    pieces = 4
    step = width // pieces
    columns = [slice(q * step, (q + 1) * step) for q in range(pieces)]
    n = lax.axis_index("node")
    l = lax.axis_index("local")
    y = l // 2
    c = lax.rem(l, 2)
    oc = 1 - c

    loads = [
        pltpu.make_async_copy(src.at[0], dst, w_sem.at[i])
        for i, (src, dst) in enumerate(((gate_hbm, gate), (up_hbm, up), (down_hbm, down)))
    ]
    for load in loads:
        load.start()

    def chip_at(step_y):
        return lax.rem(y + step_y, chips)

    def dev(node, chip, core):
        return (node, chip * 2 + core)

    barrier = pltpu.get_barrier_semaphore()
    peers = [dev(flip(n, k), y, c) for k in order if k]
    peers += [dev(flip(n, order[p]), chip_at(d), c) for p in early for d in range(1, chips)]
    peers += [dev(n, y, oc)] + [dev(n, chip_at(d), c) for d in range(1, chips)]
    for peer in peers:
        pl.semaphore_signal(barrier, inc=1, device_id=peer, device_id_type=MESH)

    ids = ids_ref[...]
    wts = wts_ref[...]
    places = nodes * slots
    place = lax.broadcasted_iota(jnp.int32, (places, rows), 0)
    first = ids[0:1, :] == place // slots
    second = ids[1:2, :] == place // slots
    named = jnp.where(first | second, 1.0, 0.0)
    before = jnp.where(
        lax.broadcasted_iota(jnp.int32, (rows, rows), 0)
        < lax.broadcasted_iota(jnp.int32, (rows, rows), 1), 1.0, 0.0,
    )
    rank = jnp.dot(named, before, preferred_element_type=jnp.float32)
    chosen = jnp.where(rank == lax.rem(place, slots).astype(jnp.float32), named, 0.0)
    weight = chosen * jnp.where(first, wts[0:1, :], wts[1:2, :])
    weight_hi = weight.astype(jnp.bfloat16)
    weight_lo = (weight - weight_hi.astype(jnp.float32)).astype(jnp.bfloat16)
    chosen = chosen.astype(jnp.bfloat16)
    for cols in columns:
        sent = jnp.dot(chosen, tok_ref[:, cols], preferred_element_type=jnp.float32)
        outgoing[:, :, cols] = sent.astype(jnp.bfloat16).reshape(nodes, slots, step)
    p_own = order.index(0)
    arrived[p_own, c, y] = outgoing[n]

    pl.semaphore_wait(barrier, len(peers))

    def remote(src, dst, s_sem, r_sem, to):
        return pltpu.make_async_remote_copy(
            src_ref=src, dst_ref=dst, send_sem=s_sem, recv_sem=r_sem,
            device_id=to, device_id_type=MESH,
        )

    started, node_queue, chip_queue, chip_queue2, node_queue2 = [], [], [], [], []
    node_window, chip_window, chip_window2, node_window2, lag, lag2 = windows

    def go(copy, queue=None, window=0):
        queue = started if queue is None else queue
        if window and len(queue) >= window:
            queue.pop(0).wait_send()
        copy.start()
        queue.append(copy)

    def node_copy(p):
        to = flip(n, order[p])
        return remote(outgoing.at[to], arrived.at[p, c, y], s_node.at[p], r_node.at[p], dev(to, y, c))

    def straight_copy(p, d):
        to = flip(n, order[p])
        return remote(
            outgoing.at[to], arrived.at[p, c, y], s_chip.at[d - 1, p], r_chip.at[d - 1, p],
            dev(to, chip_at(d), c),
        )

    def send_out(p):
        if p != p_own:
            go(node_copy(p), node_queue, node_window)
        if p in early:
            for d in range(1, chips):
                go(straight_copy(p, d))

    ahead = min(node_window + 1, nodes) if node_window else nodes
    for p in range(ahead):
        send_out(p)

    def core_copy(p):
        slab = arrived.at[p, c, y]
        return remote(slab, slab, s_core.at[p], r_core.at[p], dev(n, y, oc))

    def chip_copy(p, d):
        slab = arrived.at[p, c, y]
        return remote(slab, slab, s_chip.at[d - 1, p], r_chip.at[d - 1, p], dev(n, chip_at(d), c))

    def chip_arrival(p, d):
        slab = arrived.at[p, c, chip_at(chips - d)]
        return remote(slab, slab, s_chip.at[d - 1, p], r_chip.at[d - 1, p], dev(n, chip_at(d), c))

    def fwd_copy(p, d):
        slab = arrived.at[p, c, chip_at(chips - d)]
        return remote(slab, slab, s_fwd.at[d - 1, p], r_fwd.at[d - 1, p], dev(n, y, oc))

    def fwd_arrival(p, d):
        slab = arrived.at[p, oc, chip_at(chips - d)]
        return remote(slab, slab, s_fwd.at[d - 1, p], r_fwd.at[d - 1, p], dev(n, y, oc))

    def spread(p):
        if p != p_own:
            node_copy(p).wait_recv()
        if p not in early:
            for d in range(1, chips):
                go(chip_copy(p, d), chip_queue, chip_window)
        go(core_copy(p))

    def forward(p):
        for d in range(1, chips):
            chip_arrival(p, d).wait_recv()
            go(fwd_copy(p, d))

    def core_copy2(p):
        return remote(partial.at[p, oc], from_core.at[p], s_core2.at[p], r_core2.at[p], dev(n, y, oc))

    def compute(lo, hi):
        for p in range(lo, hi):
            slab = arrived.at[p, oc, y]
            remote(slab, slab, s_core.at[p], r_core.at[p], dev(n, y, oc)).wait_recv()
            for d in range(1, chips):
                fwd_arrival(p, d).wait_recv()
        count = (hi - lo) * 2 * chips * slots
        gated = jnp.zeros((count, units), jnp.float32)
        upward = jnp.zeros((count, units), jnp.float32)
        if lo == 0:
            loads[0].wait()
            loads[1].wait()
        for cols in columns:
            x = arrived[lo:hi, :, :, :, cols].reshape(count, step)
            gated += jnp.dot(x, gate[cols, :], preferred_element_type=jnp.float32)
            upward += jnp.dot(x, up[cols, :], preferred_element_type=jnp.float32)
        hidden[0:count] = (gated / (1.0 + jnp.exp(-gated)) * upward).astype(jnp.bfloat16)
        if lo == 0:
            loads[2].wait()
        for cols in columns:
            value = jnp.dot(hidden[0:count], down[:, cols], preferred_element_type=jnp.float32)
            partial[lo:hi, :, :, :, cols] = value.astype(jnp.bfloat16).reshape(
                hi - lo, 2, chips, slots, step
            )
        for p in way_back:
            if lo <= p < hi:
                go(core_copy2(p))

    def chip_copy2(p, d):
        return remote(
            chip_sum.at[p, d - 1], from_chip.at[p, d - 1], s_chip2.at[d - 1, p], r_chip2.at[d - 1, p],
            dev(n, chip_at(d), c),
        )

    def to_chips(p):
        core_copy2(p).wait_recv()
        for d in range(1, chips):
            other = chip_at(d)
            both = partial[p, c, other].astype(jnp.float32) + from_core[p, other].astype(jnp.float32)
            chip_sum[p, d - 1] = both.astype(jnp.bfloat16)
            go(chip_copy2(p, d), chip_queue2, chip_window2)

    def node_copy2(p):
        return remote(
            expert_out.at[p], back.at[n], s_node2.at[p], r_node2.at[p], dev(flip(n, order[p]), y, c)
        )

    def to_nodes(p):
        total = partial[p, c, y].astype(jnp.float32) + from_core[p, y].astype(jnp.float32)
        for d in range(1, chips):
            chip_copy2(p, d).wait_recv()
            total += from_chip[p, d - 1].astype(jnp.float32)
        if p == p_own:
            back[n] = total.astype(jnp.bfloat16)
        else:
            expert_out[p] = total.astype(jnp.bfloat16)
            go(node_copy2(p), node_queue2, node_window2)

    for p in range(nodes + lag):
        if p < nodes:
            spread(p)
            if p + ahead < nodes:
                send_out(p + ahead)
        if p >= lag:
            forward(p - lag)
    bounds = [(i * nodes // groups, (i + 1) * nodes // groups) for i in range(groups)]
    for lo, hi in bounds:
        compute(lo, hi)
    for i in range(nodes + lag2):
        if i < nodes:
            to_chips(way_back[i])
        if i >= lag2:
            to_nodes(way_back[i - lag2])
    for p in range(nodes):
        if p != p_own:
            src = flip(n, order[p])
            remote(
                expert_out.at[p], back.at[src], s_node2.at[p], r_node2.at[p], dev(src, y, c)
            ).wait_recv()
    over_places = (((0,), (0,)), ((), ()))
    for cols in columns:
        rows_back = back[:, :, cols].reshape(places, step)
        mixed = sum(
            lax.dot_general(part, rows_back, over_places, preferred_element_type=jnp.float32)
            for part in (weight_hi, weight_lo)
        )
        out_ref[:, cols] = mixed.astype(jnp.bfloat16)
    for copy in started + node_queue + chip_queue + chip_queue2 + node_queue2:
        copy.wait_send()


def body(nodes, chips, tokens, expert_ids, combine_weights, w_gate, w_up, w_down):
    rows, width = tokens.shape
    units = w_gate.shape[2]
    order = list(range(nodes))
    early = []
    way_back = list(reversed(range(nodes)))
    groups = 1
    windows = (0, 0, 0, 0, 2, 3)
    slab = (CAP, width)
    bf = jnp.bfloat16
    sems = pltpu.SemaphoreType.DMA
    vmem = pl.BlockSpec(memory_space=pltpu.VMEM)
    hbm = pl.BlockSpec(memory_space=pl.ANY)
    return pl.pallas_call(
        functools.partial(kernel, nodes, chips, order, early, way_back, groups, windows),
        out_shape=jax.ShapeDtypeStruct((rows, width), bf),
        in_specs=[vmem, vmem, vmem, hbm, hbm, hbm],
        out_specs=vmem,
        scratch_shapes=[
            pltpu.VMEM((width, units), bf),
            pltpu.VMEM((width, units), bf),
            pltpu.VMEM((units, width), bf),
            pltpu.VMEM((nodes,) + slab, bf),
            pltpu.VMEM((nodes, 2, chips) + slab, bf),
            pltpu.VMEM((nodes * 2 * chips * CAP, units), bf),
            pltpu.VMEM((nodes, 2, chips) + slab, bf),
            pltpu.VMEM((nodes, chips) + slab, bf),
            pltpu.VMEM((nodes, chips - 1) + slab, bf),
            pltpu.VMEM((nodes, chips - 1) + slab, bf),
            pltpu.VMEM((nodes,) + slab, bf),
            pltpu.VMEM((nodes,) + slab, bf),
            sems((3,)),
            sems((nodes,)), sems((nodes,)),
            sems((nodes,)), sems((nodes,)),
            sems((chips - 1, nodes)), sems((chips - 1, nodes)),
            sems((chips - 1, nodes)), sems((chips - 1, nodes)),
            sems((nodes,)), sems((nodes,)),
            sems((chips - 1, nodes)), sems((chips - 1, nodes)),
            sems((nodes,)), sems((nodes,)),
        ],
        compiler_params=pltpu.CompilerParams(
            collective_id=0, has_side_effects=True, vmem_limit_bytes=56 * 1024 * 1024
        ),
        name="routed_experts",
    )(tokens, expert_ids.T, combine_weights.T, w_gate, w_up, w_down)


def solution(mesh):
    nodes = mesh.shape["node"]
    chips = mesh.shape["local"] // 2
    return jax.shard_map(
        functools.partial(body, nodes, chips),
        mesh=mesh,
        in_specs=(
            P(("node", "local"), None),
            P(("node", "local"), None),
            P(("node", "local"), None),
            P("node", None, "local"),
            P("node", None, "local"),
            P("node", "local", None),
        ),
        out_specs=P(("node", "local"), None),
        check_vma=False,
    )
```

```python
import functools
import jax
import jax.numpy as jnp
from jax import lax
from jax.experimental import pallas as pl
from jax.experimental.pallas import tpu as pltpu
from jax.sharding import PartitionSpec as P

CAP = 4
MESH = pl.DeviceIdType.MESH


def flip(index, mask):
    bit = 1
    total = index
    while bit <= mask:
        if mask & bit:
            total = total + bit * (1 - 2 * lax.rem(index // bit, 2))
        bit *= 2
    return total


def kernel(
    nodes, chips, order, early, way_back, groups, windows,
    tok_ref, ids_ref, wts_ref, gate_hbm, up_hbm, down_hbm, out_ref,
    gate, up, down, outgoing, arrived, hidden, partial, from_core, chip_sum, from_chip, expert_out, back,
    w_sem, s_node, r_node, s_core, r_core, s_chip, r_chip, s_fwd, r_fwd,
    s_core2, r_core2, s_chip2, r_chip2, s_node2, r_node2,
):
    width = tok_ref.shape[1]
    rows = tok_ref.shape[0]
    units = gate.shape[1]
    slots = CAP
    pieces = 4
    step = width // pieces
    columns = [slice(q * step, (q + 1) * step) for q in range(pieces)]
    n = lax.axis_index("node")
    l = lax.axis_index("local")
    y = l // 2
    c = lax.rem(l, 2)
    oc = 1 - c

    loads = [
        pltpu.make_async_copy(src.at[0], dst, w_sem.at[i])
        for i, (src, dst) in enumerate(((gate_hbm, gate), (up_hbm, up), (down_hbm, down)))
    ]
    for load in loads:
        load.start()

    def chip_at(step_y):
        return lax.rem(y + step_y, chips)

    def dev(node, chip, core):
        return (node, chip * 2 + core)

    barrier = pltpu.get_barrier_semaphore()
    peers = [dev(flip(n, k), y, c) for k in order if k]
    peers += [dev(flip(n, order[p]), chip_at(d), c) for p in early for d in range(1, chips)]
    peers += [dev(n, y, oc)] + [dev(n, chip_at(d), c) for d in range(1, chips)]
    for peer in peers:
        pl.semaphore_signal(barrier, inc=1, device_id=peer, device_id_type=MESH)

    ids = ids_ref[...]
    wts = wts_ref[...]
    places = nodes * slots
    place = lax.broadcasted_iota(jnp.int32, (places, rows), 0)
    first = ids[0:1, :] == place // slots
    second = ids[1:2, :] == place // slots
    named = jnp.where(first | second, 1.0, 0.0)
    before = jnp.where(
        lax.broadcasted_iota(jnp.int32, (rows, rows), 0)
        < lax.broadcasted_iota(jnp.int32, (rows, rows), 1), 1.0, 0.0,
    )
    rank = jnp.dot(named, before, preferred_element_type=jnp.float32)
    chosen = jnp.where(rank == lax.rem(place, slots).astype(jnp.float32), named, 0.0)
    weight = chosen * jnp.where(first, wts[0:1, :], wts[1:2, :])
    weight_hi = weight.astype(jnp.bfloat16)
    weight_lo = (weight - weight_hi.astype(jnp.float32)).astype(jnp.bfloat16)
    chosen = chosen.astype(jnp.bfloat16)
    for cols in columns:
        sent = jnp.dot(chosen, tok_ref[:, cols], preferred_element_type=jnp.float32)
        outgoing[:, :, cols] = sent.astype(jnp.bfloat16).reshape(nodes, slots, step)
    p_own = order.index(0)
    arrived[p_own, c, y] = outgoing[n]

    pl.semaphore_wait(barrier, len(peers))

    def remote(src, dst, s_sem, r_sem, to):
        return pltpu.make_async_remote_copy(
            src_ref=src, dst_ref=dst, send_sem=s_sem, recv_sem=r_sem,
            device_id=to, device_id_type=MESH,
        )

    started, node_queue, chip_queue, chip_queue2, node_queue2 = [], [], [], [], []
    node_window, chip_window, chip_window2, node_window2, lag, lag2 = windows

    def go(copy, queue=None, window=0):
        queue = started if queue is None else queue
        if window and len(queue) >= window:
            queue.pop(0).wait_send()
        copy.start()
        queue.append(copy)

    def node_copy(p):
        to = flip(n, order[p])
        return remote(outgoing.at[to], arrived.at[p, c, y], s_node.at[p], r_node.at[p], dev(to, y, c))

    def straight_copy(p, d):
        to = flip(n, order[p])
        return remote(
            outgoing.at[to], arrived.at[p, c, y], s_chip.at[d - 1, p], r_chip.at[d - 1, p],
            dev(to, chip_at(d), c),
        )

    def send_out(p):
        if p != p_own:
            go(node_copy(p), node_queue, node_window)
        if p in early:
            for d in range(1, chips):
                go(straight_copy(p, d))

    ahead = min(node_window + 1, nodes) if node_window else nodes
    for p in range(ahead):
        send_out(p)

    def core_copy(p):
        slab = arrived.at[p, c, y]
        return remote(slab, slab, s_core.at[p], r_core.at[p], dev(n, y, oc))

    def chip_copy(p, d):
        slab = arrived.at[p, c, y]
        return remote(slab, slab, s_chip.at[d - 1, p], r_chip.at[d - 1, p], dev(n, chip_at(d), c))

    def chip_arrival(p, d):
        slab = arrived.at[p, c, chip_at(chips - d)]
        return remote(slab, slab, s_chip.at[d - 1, p], r_chip.at[d - 1, p], dev(n, chip_at(d), c))

    def fwd_copy(p, d):
        slab = arrived.at[p, c, chip_at(chips - d)]
        return remote(slab, slab, s_fwd.at[d - 1, p], r_fwd.at[d - 1, p], dev(n, y, oc))

    def fwd_arrival(p, d):
        slab = arrived.at[p, oc, chip_at(chips - d)]
        return remote(slab, slab, s_fwd.at[d - 1, p], r_fwd.at[d - 1, p], dev(n, y, oc))

    def spread(p):
        if p != p_own:
            node_copy(p).wait_recv()
        if p not in early:
            for d in range(1, chips):
                go(chip_copy(p, d), chip_queue, chip_window)
        go(core_copy(p))

    def forward(p):
        for d in range(1, chips):
            chip_arrival(p, d).wait_recv()
            go(fwd_copy(p, d))

    def core_copy2(p):
        return remote(partial.at[p, oc], from_core.at[p], s_core2.at[p], r_core2.at[p], dev(n, y, oc))

    def compute(lo, hi):
        for p in range(lo, hi):
            slab = arrived.at[p, oc, y]
            remote(slab, slab, s_core.at[p], r_core.at[p], dev(n, y, oc)).wait_recv()
            for d in range(1, chips):
                fwd_arrival(p, d).wait_recv()
        count = (hi - lo) * 2 * chips * slots
        gated = jnp.zeros((count, units), jnp.float32)
        upward = jnp.zeros((count, units), jnp.float32)
        if lo == 0:
            loads[0].wait()
            loads[1].wait()
        for cols in columns:
            x = arrived[lo:hi, :, :, :, cols].reshape(count, step)
            gated += jnp.dot(x, gate[cols, :], preferred_element_type=jnp.float32)
            upward += jnp.dot(x, up[cols, :], preferred_element_type=jnp.float32)
        hidden[0:count] = (gated / (1.0 + jnp.exp(-gated)) * upward).astype(jnp.bfloat16)
        if lo == 0:
            loads[2].wait()
        for cols in columns:
            value = jnp.dot(hidden[0:count], down[:, cols], preferred_element_type=jnp.float32)
            partial[lo:hi, :, :, :, cols] = value.astype(jnp.bfloat16).reshape(
                hi - lo, 2, chips, slots, step
            )
        for p in way_back:
            if lo <= p < hi:
                go(core_copy2(p))

    def chip_copy2(p, d):
        return remote(
            chip_sum.at[p, d - 1], from_chip.at[p, d - 1], s_chip2.at[d - 1, p], r_chip2.at[d - 1, p],
            dev(n, chip_at(d), c),
        )

    def to_chips(p):
        core_copy2(p).wait_recv()
        for d in range(1, chips):
            other = chip_at(d)
            both = partial[p, c, other].astype(jnp.float32) + from_core[p, other].astype(jnp.float32)
            chip_sum[p, d - 1] = both.astype(jnp.bfloat16)
            go(chip_copy2(p, d), chip_queue2, chip_window2)

    def node_copy2(p):
        return remote(
            expert_out.at[p], back.at[n], s_node2.at[p], r_node2.at[p], dev(flip(n, order[p]), y, c)
        )

    def to_nodes(p):
        total = partial[p, c, y].astype(jnp.float32) + from_core[p, y].astype(jnp.float32)
        for d in range(1, chips):
            chip_copy2(p, d).wait_recv()
            total += from_chip[p, d - 1].astype(jnp.float32)
        if p == p_own:
            back[n] = total.astype(jnp.bfloat16)
        else:
            expert_out[p] = total.astype(jnp.bfloat16)
            go(node_copy2(p), node_queue2, node_window2)

    for p in range(nodes + lag):
        if p < nodes:
            spread(p)
            if p + ahead < nodes:
                send_out(p + ahead)
        if p >= lag:
            forward(p - lag)
    bounds = [(i * nodes // groups, (i + 1) * nodes // groups) for i in range(groups)]
    for lo, hi in bounds:
        compute(lo, hi)
    for i in range(nodes + lag2):
        if i < nodes:
            to_chips(way_back[i])
        if i >= lag2:
            to_nodes(way_back[i - lag2])
    for p in range(nodes):
        if p != p_own:
            src = flip(n, order[p])
            remote(
                expert_out.at[p], back.at[src], s_node2.at[p], r_node2.at[p], dev(src, y, c)
            ).wait_recv()
    over_places = (((0,), (0,)), ((), ()))
    for cols in columns:
        rows_back = back[:, :, cols].reshape(places, step)
        mixed = sum(
            lax.dot_general(part, rows_back, over_places, preferred_element_type=jnp.float32)
            for part in (weight_hi, weight_lo)
        )
        out_ref[:, cols] = mixed.astype(jnp.bfloat16)
    for copy in started + node_queue + chip_queue + chip_queue2 + node_queue2:
        copy.wait_send()


def body(nodes, chips, tokens, expert_ids, combine_weights, w_gate, w_up, w_down):
    rows, width = tokens.shape
    units = w_gate.shape[2]
    order = list(range(nodes))
    early = []
    half = nodes // 2
    way_back = [p - i for i in range(half) for p in (nodes - 1, half - 1)]
    groups = 1
    windows = (0, 0, 0, 0, 2, 3)
    slab = (CAP, width)
    bf = jnp.bfloat16
    sems = pltpu.SemaphoreType.DMA
    vmem = pl.BlockSpec(memory_space=pltpu.VMEM)
    hbm = pl.BlockSpec(memory_space=pl.ANY)
    return pl.pallas_call(
        functools.partial(kernel, nodes, chips, order, early, way_back, groups, windows),
        out_shape=jax.ShapeDtypeStruct((rows, width), bf),
        in_specs=[vmem, vmem, vmem, hbm, hbm, hbm],
        out_specs=vmem,
        scratch_shapes=[
            pltpu.VMEM((width, units), bf),
            pltpu.VMEM((width, units), bf),
            pltpu.VMEM((units, width), bf),
            pltpu.VMEM((nodes,) + slab, bf),
            pltpu.VMEM((nodes, 2, chips) + slab, bf),
            pltpu.VMEM((nodes * 2 * chips * CAP, units), bf),
            pltpu.VMEM((nodes, 2, chips) + slab, bf),
            pltpu.VMEM((nodes, chips) + slab, bf),
            pltpu.VMEM((nodes, chips - 1) + slab, bf),
            pltpu.VMEM((nodes, chips - 1) + slab, bf),
            pltpu.VMEM((nodes,) + slab, bf),
            pltpu.VMEM((nodes,) + slab, bf),
            sems((3,)),
            sems((nodes,)), sems((nodes,)),
            sems((nodes,)), sems((nodes,)),
            sems((chips - 1, nodes)), sems((chips - 1, nodes)),
            sems((chips - 1, nodes)), sems((chips - 1, nodes)),
            sems((nodes,)), sems((nodes,)),
            sems((chips - 1, nodes)), sems((chips - 1, nodes)),
            sems((nodes,)), sems((nodes,)),
        ],
        compiler_params=pltpu.CompilerParams(
            collective_id=0, has_side_effects=True, vmem_limit_bytes=56 * 1024 * 1024
        ),
        name="routed_experts",
    )(tokens, expert_ids.T, combine_weights.T, w_gate, w_up, w_down)


def solution(mesh):
    nodes = mesh.shape["node"]
    chips = mesh.shape["local"] // 2
    return jax.shard_map(
        functools.partial(body, nodes, chips),
        mesh=mesh,
        in_specs=(
            P(("node", "local"), None),
            P(("node", "local"), None),
            P(("node", "local"), None),
            P("node", None, "local"),
            P("node", None, "local"),
            P("node", "local", None),
        ),
        out_specs=P(("node", "local"), None),
        check_vma=False,
    )
```
